128 devices in a mesh: row: 4 (over y), col: 32 (over x, z, core).
Axes of the slice: x: 4, y: 4, z: 4, core: 2. Of those that a mesh axis runs over, the one named last changes fastest.
Arguments:
- tokens: bfloat16 [16384, 1024], P(('row', 'col')), may hold values from -6 to 6
- lengths: int32 [128, 4], P(('row', 'col')), may hold values from 1 to 64, 128 in all within a row
- mixer_in: bfloat16 [1024, 4120], replicated, may hold values from -0.1875 to 0.1875
- conv_weight: float32 [4, 1792], replicated, may hold values from -3 to 3
- conv_bias: float32 [1792], replicated, may hold values from -3 to 3
- step_bias: float32 [24], replicated, may hold values from -3 to -1
- decay_log: float32 [24], replicated, may hold values from -4 to 2.5
- skip_gain: float32 [24], replicated, may hold values from 0.5 to 1.5
- ssm_gain: float32 [1536], replicated, may hold values from 0.5 to 1.5
- gain_in: float32 [1024], replicated, may hold values from 0.5 to 1.5
- mixer_out: bfloat16 [2048, 1024], replicated, may hold values from -0.1875 to 0.1875
- gain_mlp: float32 [1024], replicated, may hold values from 0.5 to 1.5
- w_gate: bfloat16 [1024, 2048], P('row', 'col'), may hold values from -0.1875 to 0.1875
- w_up: bfloat16 [1024, 2048], P('row', 'col'), may hold values from -0.1875 to 0.1875
- w_down: bfloat16 [2048, 1024], P('col', 'row'), may hold values from -0.125 to 0.125
- cotangent: bfloat16 [16384, 1024], P(('row', 'col')), may hold values from -6 to 6
Outputs:
- output: bfloat16 [16384, 1024], P(('row', 'col'))
- d_tokens: float32 [16384, 1024], P(('row', 'col'))
- grad_mixer_in: float32 [1024, 4120], P(('row', 'col'))
- grad_conv_weight: float32 [4, 1792], replicated
- grad_conv_bias: float32 [1792], replicated
- grad_step_bias: float32 [24], replicated
- grad_decay_log: float32 [24], replicated
- grad_skip_gain: float32 [24], replicated
- grad_ssm_gain: float32 [1536], replicated
- grad_gain_in: float32 [1024], replicated
- grad_mixer_out: float32 [2048, 1024], P(('row', 'col'))
- grad_gain_mlp: float32 [1024], replicated
- grad_w_gate: float32 [1024, 2048], P('row', 'col')
- grad_w_up: float32 [1024, 2048], P('row', 'col')
- grad_w_down: float32 [2048, 1024], P('col', 'row')
The draws below stay inside these ranges and needn't reach their ends.
Inputs may be any that keep to these rules, and one draw needn't show every extreme that they name: Each row holds the lengths of the sequences on one device in order; they sum to 128, and the largest in each row is exactly 64.
All inputs are finite; a program needn't handle non-finite values.
Results may differ from the reference program's by a relative error of at most 0.018.
Values may be sent and summed in bfloat16 or wider, within the bound.
No kernel may reach another device: no remote copies, remote signals or barrier semaphores. Data moves between devices by JAX's collectives and lax.ppermute only.
A program may use at most 256 MiB of HBM per device.

```python
import math
import jax
import jax.numpy as jnp
import numpy as np
from jax import lax

D = 1024
NH = 24
HEAD_SIZE = 64
NS = 128
QUERY_HEADS = 8
KEY_VALUE_HEADS = 2
FF = 2048
KCONV = 4
TOK_DEV = 128
SEQ_DEV = 4
TOKENS = 16384
CONVW = 1792
PROJ = 4120
MIXW = 2048
N_ROW = 4
N_COL = 32


def block_scale(own_key, shape, shards, smallest, top_value):
    level, own = 1.0, jax.random.fold_in(own_key, 6)
    for dim, shards_of in shards:
        heights = jnp.exp(jax.random.uniform(jax.random.fold_in(own, dim), (shards_of,), jnp.float32, smallest / len(shards), top_value / len(shards)))
        level = level * jnp.repeat(heights, shape[dim] // shards_of).reshape([-1 if axis == dim else 1 for axis in range(len(shape))])
    return level


def profile(amount, total, limit, skew):
    portions = [(1 << 20) // math.isqrt(grade ** skew) + 1 for grade in range(2, amount + 1)]
    spare, given = total - limit - (amount - 1), [1] * (amount - 1)
    while spare > 0:
        free = [i for i in range(amount - 1) if given[i] < limit]
        mass, budget = sum([portions[i] for i in free]), spare
        for i in free:
            more = min(limit - given[i], max(1, budget * portions[i] // mass), spare)
            given[i] = given[i] + more
            spare = spare - more
    return np.array([limit] + given)


def ragged(stream_key, number_of, total, limit, slope):
    if number_of == 2:
        one = jax.random.randint(stream_key, (), max(1, total - limit), min(limit, total - 1) + 1)
        return jnp.stack([one, total - one])
    tallies = jnp.asarray(profile(number_of, total, limit, slope), jnp.int32)
    twos = (number_of - 1) // 2
    giver, sink = tallies[1:1 + 2 * twos:2], tallies[2:2 + 2 * twos:2]
    margin = jnp.minimum(giver - 1, limit - sink)
    passed = jax.random.randint(jax.random.fold_in(stream_key, 1), (twos,), 0, 1 << 20) % (margin + 1)
    tallies = tallies.at[1:1 + 2 * twos:2].set(giver - passed).at[2:2 + 2 * twos:2].set(sink + passed)
    return tallies[jax.random.permutation(jax.random.fold_in(stream_key, 2), number_of)]


def noise(key, dims, scale, limit, pieces=(), kind=jnp.bfloat16):
    drawn = scale * jax.random.normal(key, dims, jnp.float32)
    if pieces:
        drawn = drawn * block_scale(key, dims, pieces, -0.22, 0.18)
    return jnp.clip(drawn, -limit, limit).astype(kind)


def setup_inputs(seed: int = 0) -> dict:
    keys = jax.random.split(jax.random.key(seed), 17)
    return {
        "tokens": noise(keys[0], (TOKENS, D), 1.0, 6.0, ((0, 128),)),
        "lengths": jax.vmap(lambda own: ragged(own, SEQ_DEV, TOK_DEV, TOK_DEV // 2, 2))(jax.random.split(keys[1], (N_ROW * N_COL))).reshape((N_ROW * N_COL, SEQ_DEV)).astype(jnp.int32),
        "mixer_in": noise(keys[2], (D, PROJ), D ** -0.5, 0.1875),
        "conv_weight": noise(keys[3], (KCONV, CONVW), 0.5, 3.0, (), jnp.float32),
        "conv_bias": noise(keys[4], (CONVW,), 0.3, 3.0, (), jnp.float32),
        "step_bias": jnp.clip(jax.random.uniform(keys[5], (NH,), jnp.float32, -3.0, -1.0), -3.0, -1.0),
        "decay_log": jnp.clip(jax.random.uniform(keys[6], (NH,), jnp.float32, -4.0, 2.5), -4.0, 2.5),
        "skip_gain": jnp.clip(jax.random.uniform(keys[7], (NH,), jnp.float32, 0.5, 1.5), 0.5, 1.5),
        "ssm_gain": jnp.clip(1.0 + 0.1 * jax.random.normal(keys[8], (NH * HEAD_SIZE,), jnp.float32), 0.5, 1.5),
        "gain_in": jnp.clip(1.0 + 0.1 * jax.random.normal(keys[9], (D,), jnp.float32), 0.5, 1.5),
        "mixer_out": noise(keys[10], (MIXW, D), D ** -0.5, 0.1875),
        "gain_mlp": jnp.clip(1.0 + 0.1 * jax.random.normal(keys[11], (D,), jnp.float32), 0.5, 1.5),
        "w_gate": noise(keys[12], (D, FF), D ** -0.5, 0.1875, ((0, 4), (1, 32))),
        "w_up": noise(keys[13], (D, FF), D ** -0.5, 0.1875, ((0, 4), (1, 32))),
        "w_down": noise(keys[14], (FF, D), FF ** -0.5, 0.125, ((0, 32), (1, 4))),
        "cotangent": noise(keys[15], (TOKENS, D), 1.0, 6.0, ((0, 128),)),
    }


norm_eps = 1e-05
rope_base = 100000000000.0
highest = lax.Precision.HIGHEST

@jax.custom_vjp
def low(v):
    return lax.optimization_barrier(v.astype(jnp.bfloat16)).astype(jnp.float32)

@jax.custom_vjp
def low_back(v):
    return v

def low_keep(v):
    return (low(v), None)

def low_pass(kept, grad):
    return (grad,)

def back_keep(v):
    return (v, None)

def back_low(kept, grad):
    return (low(grad),)
low.defvjp(low_keep, low_pass)
low_back.defvjp(back_keep, back_low)

def rms_norm(values, gain):
    return values * lax.rsqrt(lax.optimization_barrier(jnp.mean(values * values, axis=-1, keepdims=True)) + norm_eps) * gain

def layout(lens, token_count):
    ends = jnp.cumsum(lens).astype(jnp.int32)
    places = jnp.arange(token_count, dtype=jnp.int32)
    after = (places[:, None] >= ends[None, :]).astype(jnp.int32)
    segment = lax.optimization_barrier(jnp.sum(after, axis=1)).astype(jnp.int32)
    first = lax.optimization_barrier(jnp.sum(after * lens[None, :], axis=1)).astype(jnp.int32)
    return (segment, places - first)

def rotary_apply(values, cosine_table, sine_table):
    half = values.shape[-1] // 2
    front = values[..., :half]
    back = values[..., half:]
    return jnp.concatenate([front * cosine_table - back * sine_table, back * cosine_table + front * sine_table], axis=-1)

def mixer_block(x, segment, position, w_in, conv_weight, conv_bias, step_bias, decay_log, skip_gain, ssm_gain, gain_in, w_out):
    token_count = x.shape[0]
    inner = NH * HEAD_SIZE
    width = inner + 2 * NS
    places = jnp.arange(token_count, dtype=jnp.int32)
    normed = low(rms_norm(x, gain_in))
    projected = low_back(jnp.dot(normed, w_in, precision=highest))
    out_gate = projected[:, :inner]
    conv_in = projected[:, inner:inner + width]
    step_in = projected[:, inner + width:inner + width + NH]
    attention_input = projected[:, inner + width + NH:]
    query_rows = attention_input[:, :QUERY_HEADS * HEAD_SIZE].reshape(token_count, QUERY_HEADS, HEAD_SIZE)
    every_key = attention_input[:, QUERY_HEADS * HEAD_SIZE:(QUERY_HEADS + KEY_VALUE_HEADS) * HEAD_SIZE].reshape(token_count, KEY_VALUE_HEADS, HEAD_SIZE)
    every_value = attention_input[:, (QUERY_HEADS + KEY_VALUE_HEADS) * HEAD_SIZE:].reshape(token_count, KEY_VALUE_HEADS, HEAD_SIZE)
    taps = conv_weight.shape[0]
    summed = conv_bias + conv_weight[taps - 1] * conv_in
    for offset in range(1, taps):
        earlier = jnp.concatenate([jnp.zeros((offset, width), jnp.float32), conv_in[:token_count - offset]], axis=0)
        prior_segment = jnp.concatenate([jnp.full((offset,), -1, jnp.int32), segment[:token_count - offset]])
        keep = (prior_segment == segment).astype(jnp.float32)[:, None]
        summed = summed + conv_weight[taps - 1 - offset] * earlier * keep
    active = jax.nn.silu(summed)
    heads_in = active[:, :inner].reshape(token_count, NH, HEAD_SIZE)
    state_in = active[:, inner:inner + NS]
    state_out = active[:, inner + NS:]
    delta = jax.nn.softplus(step_in + step_bias)
    running = jnp.cumsum(-delta * jnp.exp(decay_log), axis=0)
    allowed = (places[:, None] >= places[None, :]) & (segment[:, None] == segment[None, :])
    spread = running.T[:, :, None] - running.T[:, None, :]
    decay = jnp.where(allowed[None], jnp.exp(jnp.where(allowed[None], spread, 0.0)), 0.0)
    intersection = jnp.dot(state_out, state_in.T, precision=highest)
    mixing = intersection[None] * decay * delta.T[:, None, :]
    states = jnp.einsum('hts,shp->thp', mixing, heads_in, precision=highest) + skip_gain[None, :, None] * heads_in
    gated = states.reshape(token_count, inner) * jax.nn.silu(out_gate)
    ssm_out = rms_norm(gated, ssm_gain)
    half = HEAD_SIZE // 2
    frequency = rope_base ** (-jnp.arange(half, dtype=jnp.float32) / half)
    angles = position.astype(jnp.float32)[:, None] * frequency[None, :]
    cosine_table = jnp.cos(angles)[:, None, :]
    sine_table = jnp.sin(angles)[:, None, :]
    rotated_query = rotary_apply(query_rows, cosine_table, sine_table).reshape(token_count, KEY_VALUE_HEADS, QUERY_HEADS // KEY_VALUE_HEADS, HEAD_SIZE)
    turned_k = rotary_apply(every_key, cosine_table, sine_table)
    scores = jnp.einsum('tkgd,skd->kgts', rotated_query, turned_k, precision=highest) / math.sqrt(HEAD_SIZE)
    scores = jnp.where(allowed[None, None], scores, -1e+30)
    attention_weights = jax.nn.softmax(scores, axis=-1)
    attended = jnp.einsum('kgts,skd->tkgd', attention_weights, every_value, precision=highest).reshape(token_count, QUERY_HEADS * HEAD_SIZE)
    joined = low(jnp.concatenate([ssm_out, attended], axis=1))
    return x + low_back(jnp.dot(joined, w_out, precision=highest))

def layer_block(x, lens, w_in, conv_weight, conv_bias, step_bias, decay_log, skip_gain, ssm_gain, gain_in, w_out, gain_mlp, w_gate, w_up, w_down):
    segment, position = layout(lens, x.shape[0])
    mixed = mixer_block(x, segment, position, w_in, conv_weight, conv_bias, step_bias, decay_log, skip_gain, ssm_gain, gain_in, w_out)
    normed = low(rms_norm(mixed, gain_mlp))
    paired = low_back(jnp.dot(normed, jnp.concatenate([w_gate, w_up], axis=1), precision=highest))
    hidden = low(jax.nn.silu(paired[:, :FF]) * paired[:, FF:])
    return mixed + jnp.dot(hidden, w_down, precision=highest)

def reference(tokens, lengths, mixer_in, conv_weight, conv_bias, step_bias, decay_log, skip_gain, ssm_gain, gain_in, mixer_out, gain_mlp, w_gate, w_up, w_down, cotangent):

    def whole(x, w_in, kernel, kernel_bias, bias_step, log_decay, gain_skip, gain_ssm, gain_first, w_out, gain_second, gate_w, up_w, down_w):
        blocks = x.reshape(N_ROW * N_COL, TOK_DEV, D)

        def one_block(pair):
            return layer_block(pair[0], pair[1], w_in, kernel, kernel_bias, bias_step, log_decay, gain_skip, gain_ssm, gain_first, w_out, gain_second, gate_w, up_w, down_w)
        result = lax.map(jax.checkpoint(one_block), (blocks, lengths))
        return result.reshape(TOKENS, D)
    params = [a.astype(jnp.float32) for a in (tokens, mixer_in, conv_weight, conv_bias, step_bias, decay_log, skip_gain, ssm_gain, gain_in, mixer_out, gain_mlp, w_gate, w_up, w_down)]
    output, pullback = jax.vjp(whole, *params)
    grads = pullback(cotangent.astype(jnp.float32))
    return (output.astype(jnp.bfloat16), grads[0], grads[1], grads[2], grads[3], grads[4], grads[5], grads[6], grads[7], grads[8], grads[9], grads[10], grads[11], grads[12], grads[13])
```

```python
import math

import jax
import jax.numpy as jnp
from jax import lax
from jax.experimental import pallas as pl
from jax.experimental.pallas import tpu as pltpu
from jax.sharding import Mesh, PartitionSpec as P

NH = 24
HEAD_SIZE = 64
NS = 128
QUERY_HEADS = 8
KEY_VALUE_HEADS = 2
INNER = NH * HEAD_SIZE
CONVW = INNER + 2 * NS
QKV = (QUERY_HEADS + 2 * KEY_VALUE_HEADS) * HEAD_SIZE

norm_eps = 1e-05
rope_base = 100000000000.0
f32 = jnp.float32
bf16 = jnp.bfloat16

ALL = ("y", "x", "z", "core")
CHIPS = ("y", "x", "z")
COL = ("x", "z", "core")
AXIS = 4


def moved(array, axis, shift):
    size = lax.axis_size(axis)
    return lax.ppermute(array, axis, [(i, (i + shift) % size) for i in range(size)])


def turned(array, axis, dim):
    twice = jnp.concatenate([array, array], axis=dim)
    return lax.dynamic_slice_in_dim(twice, lax.axis_index(axis), AXIS, axis=dim)


def added(first, others):
    total = first.astype(f32)
    for o in others:
        total = total + o.astype(f32)
    return total


def rms_norm(values, gain):
    return values * lax.rsqrt(jnp.mean(values * values, axis=-1, keepdims=True) + norm_eps) * gain


def layout(lens, token_count):
    ends = jnp.cumsum(lens)
    places = jnp.arange(token_count, dtype=jnp.int32)
    after = (places[:, None] >= ends[None, :]).astype(jnp.int32)
    segment = jnp.sum(after, axis=1)
    first = jnp.sum(after * lens[None, :], axis=1)
    return (segment, places - first)


def rotary_apply(values, cosine_table, sine_table):
    half = values.shape[-1] // 2
    front = values[..., :half]
    back = values[..., half:]
    return jnp.concatenate(
        [front * cosine_table - back * sine_table, back * cosine_table + front * sine_table],
        axis=-1,
    )


def mixer_core(
    out_gate,
    conv_in,
    step_in,
    attention_input,
    segment,
    position,
    conv_weight,
    conv_bias,
    step_bias,
    decay_log,
    skip_gain,
    ssm_gain,
):
    token_count = out_gate.shape[0]
    inner = INNER
    width = CONVW
    places = jnp.arange(token_count, dtype=jnp.int32)
    query_rows = attention_input[:, : QUERY_HEADS * HEAD_SIZE].reshape(
        token_count, QUERY_HEADS, HEAD_SIZE
    )
    every_key = attention_input[
        :, QUERY_HEADS * HEAD_SIZE : (QUERY_HEADS + KEY_VALUE_HEADS) * HEAD_SIZE
    ].reshape(token_count, KEY_VALUE_HEADS, HEAD_SIZE)
    every_value = attention_input[:, (QUERY_HEADS + KEY_VALUE_HEADS) * HEAD_SIZE :].reshape(
        token_count, KEY_VALUE_HEADS, HEAD_SIZE
    )
    taps = conv_weight.shape[0]
    summed = conv_bias + conv_weight[taps - 1] * conv_in
    for offset in range(1, taps):
        earlier = jnp.concatenate(
            [jnp.zeros((offset, width), jnp.float32), conv_in[: token_count - offset]], axis=0
        )
        prior_segment = jnp.concatenate(
            [jnp.full((offset,), -1, jnp.int32), segment[: token_count - offset]]
        )
        keep = (prior_segment == segment).astype(jnp.float32)[:, None]
        summed = summed + conv_weight[taps - 1 - offset] * earlier * keep
    active = jax.nn.silu(summed)
    heads_in = active[:, :inner].reshape(token_count, NH, HEAD_SIZE)
    state_in = active[:, inner : inner + NS]
    state_out = active[:, inner + NS :]
    delta = jax.nn.softplus(step_in + step_bias)
    running = jnp.cumsum(-delta * jnp.exp(decay_log), axis=0)
    allowed = (places[:, None] >= places[None, :]) & (segment[:, None] == segment[None, :])
    spread = running.T[:, :, None] - running.T[:, None, :]
    decay = jnp.where(allowed[None], jnp.exp(jnp.where(allowed[None], spread, 0.0)), 0.0)
    intersection = jnp.dot(state_out, state_in.T)
    mixing = intersection[None] * decay * delta.T[:, None, :]
    states = jnp.einsum("hts,shp->thp", mixing, heads_in) + skip_gain[None, :, None] * heads_in
    gated = states.reshape(token_count, inner) * jax.nn.silu(out_gate)
    ssm_out = rms_norm(gated, ssm_gain)
    half = HEAD_SIZE // 2
    frequency = rope_base ** (-jnp.arange(half, dtype=jnp.float32) / half)
    angles = position.astype(jnp.float32)[:, None] * frequency[None, :]
    cosine_table = jnp.cos(angles)[:, None, :]
    sine_table = jnp.sin(angles)[:, None, :]
    rotated_query = rotary_apply(query_rows, cosine_table, sine_table).reshape(
        token_count, KEY_VALUE_HEADS, QUERY_HEADS // KEY_VALUE_HEADS, HEAD_SIZE
    )
    turned_k = rotary_apply(every_key, cosine_table, sine_table)
    scores = jnp.einsum("tkgd,skd->kgts", rotated_query, turned_k) / math.sqrt(HEAD_SIZE)
    scores = jnp.where(allowed[None, None], scores, -1e30)
    attention_weights = jax.nn.softmax(scores, axis=-1)
    attended = jnp.einsum("kgts,skd->tkgd", attention_weights, every_value).reshape(
        token_count, QUERY_HEADS * HEAD_SIZE
    )
    return jnp.concatenate([ssm_out, attended], axis=1)


def dot_nn(left, right):
    return lax.dot_general(left, right, (((1,), (0,)), ((), ())), preferred_element_type=f32)


def dot_nt(left, right):
    return lax.dot_general(left, right, (((1,), (1,)), ((), ())), preferred_element_type=f32)


def dot_tn(left, right):
    return lax.dot_general(left, right, (((0,), (0,)), ((), ())), preferred_element_type=f32)


FF_BLOCK = 256


def ffn_body(x_ref, ct_ref, w_ref, out_ref, dn_ref, dw_ref):
    @pl.when(pl.program_id(0) == 0)
    def _():
        out_ref[...] = jnp.zeros_like(out_ref)
        dn_ref[...] = jnp.zeros_like(dn_ref)

    x = x_ref[...]
    ct = ct_ref[...]
    chunks = w_ref.shape[0]
    part = w_ref.shape[2] // 3
    gate, up, d_hidden = 0.0, 0.0, 0.0
    for c in range(chunks):
        cols = slice(c * part, (c + 1) * part)
        gate = gate + dot_nt(x[:, cols], w_ref[c, :, :part])
        up = up + dot_nt(x[:, cols], w_ref[c, :, part : 2 * part])
        d_hidden = d_hidden + dot_nt(ct[:, cols], w_ref[c, :, 2 * part :])
    sigma = jax.nn.sigmoid(gate)
    silu = gate * sigma
    hidden = (silu * up).astype(bf16)
    d_gate = (d_hidden * up * sigma * (1.0 + gate * (1.0 - sigma))).astype(bf16)
    d_up = (d_hidden * silu).astype(bf16)
    dw_gate = dot_tn(d_gate, x).astype(bf16)
    dw_up = dot_tn(d_up, x).astype(bf16)
    dw_down = dot_tn(hidden, ct).astype(bf16)
    for c in range(chunks):
        cols = slice(c * part, (c + 1) * part)
        out_ref[:, cols] += dot_nn(hidden, w_ref[c, :, 2 * part :])
        dn_ref[:, cols] += dot_nn(d_gate, w_ref[c, :, :part]) + dot_nn(
            d_up, w_ref[c, :, part : 2 * part]
        )
        at = 3 * c * part
        dw_ref[:, at : at + part] = dw_gate[:, cols]
        dw_ref[:, at + part : at + 2 * part] = dw_up[:, cols]
        dw_ref[:, at + 2 * part : at + 3 * part] = dw_down[:, cols]


def feed_forward(x, ct, weights):
    chunks, units, wide = weights.shape
    tokens, width = x.shape
    whole = pl.BlockSpec((tokens, width), lambda i: (0, 0))
    return pl.pallas_call(
        ffn_body,
        grid=(units // FF_BLOCK,),
        in_specs=[whole, whole, pl.BlockSpec((chunks, FF_BLOCK, wide), lambda i: (0, i, 0))],
        out_specs=[whole, whole, pl.BlockSpec((FF_BLOCK, chunks * wide), lambda i: (i, 0))],
        out_shape=[
            jax.ShapeDtypeStruct((tokens, width), f32),
            jax.ShapeDtypeStruct((tokens, width), f32),
            jax.ShapeDtypeStruct((units, chunks * wide), bf16),
        ],
        compiler_params=pltpu.CompilerParams(vmem_limit_bytes=48 * 1024 * 1024),
        cost_estimate=pl.CostEstimate(
            flops=18 * tokens * width * units,
            bytes_accessed=4 * chunks * units * wide,
            transcendentals=tokens * units,
        ),
        name="feed_forward",
    )(x, ct, weights)


SMALL_WIDE = 1920


def local(
    tokens,
    lengths,
    mixer_in,
    conv_weight,
    conv_bias,
    step_bias,
    decay_log,
    skip_gain,
    ssm_gain,
    gain_in,
    mixer_out,
    gain_mlp,
    w_gate,
    w_up,
    w_down,
    cotangent,
):
    token_count, width = tokens.shape
    core = lax.axis_index("core")

    own = jnp.concatenate([w_gate.T, w_up.T, w_down], axis=1)
    weights = lax.all_gather(own, ALL, tiled=True).reshape(AXIS, -1, own.shape[1])

    segment, position = layout(lengths[0], token_count)
    first_in = tokens.astype(f32)
    normed_first, first_pull = jax.vjp(rms_norm, first_in, gain_in)
    normed_first_low = normed_first.astype(bf16)
    projected = jnp.dot(normed_first_low, mixer_in, preferred_element_type=f32)

    def core_local(out_gate, conv_in, step_in, qkv, *params):
        return mixer_core(out_gate, conv_in, step_in, qkv, segment, position, *params)

    joined_wide, core_pull = jax.vjp(
        core_local,
        projected[:, :INNER],
        projected[:, INNER : INNER + CONVW],
        projected[:, INNER + CONVW : INNER + CONVW + NH],
        projected[:, INNER + CONVW + NH :],
        conv_weight,
        conv_bias,
        step_bias,
        decay_log,
        skip_gain,
        ssm_gain,
    )
    joined = joined_wide.astype(bf16)
    mixed = first_in + jnp.dot(joined, mixer_out, preferred_element_type=f32)
    normed_mlp, norm_pull = jax.vjp(rms_norm, mixed, gain_mlp)
    ffn_out, d_normed, d_weights = feed_forward(normed_mlp.astype(bf16), cotangent, weights)
    output = (mixed + ffn_out).astype(bf16)

    ff = lax.psum_scatter(d_weights, COL, scatter_dimension=0, tiled=True)
    ff = turned(ff.reshape(ff.shape[0], AXIS, -1).swapaxes(0, 1), "y", 0)
    ff = added(ff[0], [moved(ff[k], "y", k) for k in range(1, AXIS)])
    part = ff.shape[1] // 3

    d_mixed, d_gain_mlp = norm_pull(d_normed)
    d_mixed = d_mixed + cotangent.astype(f32)
    d_term = d_mixed.astype(bf16)

    by_place = joined.T.reshape(AXIS**3, 2, -1, token_count).swapaxes(0, 1)
    theirs = lax.dynamic_index_in_dim(by_place, 1 - core, 0, False)
    mine = lax.dynamic_index_in_dim(by_place, core, 0, False)
    got = moved(jnp.dot(theirs.reshape(-1, token_count), d_term, preferred_element_type=f32).astype(bf16), "core", 1)
    out_sum = added(jnp.dot(mine.reshape(-1, token_count), d_term, preferred_element_type=f32), [got])
    out_sum = out_sum.astype(bf16).reshape(AXIS**3, -1, width)
    out_parts = lax.all_to_all(out_sum, CHIPS, 0, 0, tiled=True)
    grad_out = jnp.sum(out_parts.astype(f32), axis=0)

    d_joined = dot_nt(d_term, mixer_out)
    d_gate, d_conv, d_step, d_qkv, *d_params = core_pull(d_joined)
    d_gate, d_conv, d_step, d_qkv = (a.astype(bf16) for a in (d_gate, d_conv, d_step, d_qkv))
    d_projected = jnp.concatenate([d_gate, d_conv, d_step, d_qkv], axis=1)
    d_normed_first = dot_nt(d_projected, mixer_in)
    d_first, d_gain_in = first_pull(d_normed_first)
    d_tokens = d_mixed + d_first

    lefts = normed_first_low.T.reshape(AXIS, AXIS, AXIS, 2, -1, token_count)
    for dim, axis in enumerate(CHIPS):
        lefts = turned(lefts, axis, dim)
    groups = []
    spare = SMALL_WIDE - CONVW - NH
    rights = (
        jnp.concatenate([d_gate, d_qkv], axis=1),
        jnp.concatenate([d_conv, jnp.pad(d_step, ((0, 0), (0, spare)))], axis=1),
    )
    smalls = [*d_params, d_gain_in, d_gain_mlp]
    small = jnp.concatenate([s.ravel() for s in smalls])
    small = jnp.pad(small, (0, 8 * SMALL_WIDE - small.size)).reshape(8, SMALL_WIDE)
    small = lax.optimization_barrier(small.astype(bf16))
    small = added(small, [moved(small, "core", 1)])
    sums = []
    for right, order in zip(rights, ((3, 1, 2, 0, 4, 5), (3, 2, 1, 0, 4, 5))):
        left = lefts.transpose(order)
        theirs = lax.dynamic_index_in_dim(left, 1 - core, 0, False)
        mine = lax.dynamic_index_in_dim(left, core, 0, False)
        rows = theirs.size // AXIS // token_count
        got = moved(
            jnp.dot(theirs.reshape(-1, token_count), right, preferred_element_type=f32).astype(bf16), "core", 1
        ).reshape(AXIS, rows, -1)
        sums.append(
            [
                added(jnp.dot(mine[k].reshape(rows, token_count), right, preferred_element_type=f32), [got[k]]).astype(bf16)
                for k in range(AXIS)
            ]
        )
    a, b = sums
    small = lax.optimization_barrier(small.astype(bf16))
    a_in = [moved(a[k], "x", k) for k in range(1, AXIS)]
    b_in = [moved(jnp.concatenate([b[k], small]), "z", k) for k in range(1, AXIS)]
    small = (small.astype(f32) + b_in[1][-8:].astype(f32)) + (b_in[0][-8:].astype(f32) + b_in[2][-8:].astype(f32))
    rows = a[0].shape[0] // AXIS
    a = [added(a[0][k * rows : (k + 1) * rows], [r[k * rows : (k + 1) * rows] for r in a_in]).astype(bf16) for k in range(AXIS)]
    b = [added(b[0][k * rows : (k + 1) * rows], [r[k * rows : (k + 1) * rows] for r in b_in]).astype(bf16) for k in range(AXIS)]
    small = lax.optimization_barrier(small.astype(bf16))
    a_in = [moved(a[k], "z", k) for k in range(1, AXIS)]
    b_in = [moved(jnp.concatenate([b[k], small]), "x", k) for k in range(1, AXIS)]
    small = (small.astype(f32) + b_in[1][-8:].astype(f32)) + (b_in[0][-8:].astype(f32) + b_in[2][-8:].astype(f32))
    small = lax.optimization_barrier(small.astype(bf16))
    rows = rows // AXIS
    both = []
    for k in range(AXIS):
        at = slice(k * rows, (k + 1) * rows)
        both.append(
            jnp.concatenate(
                [
                    added(a[0][at], [r[at] for r in a_in]).astype(bf16),
                    added(b[0][at], [r[at] for r in b_in]).astype(bf16),
                    small,
                ],
                axis=1,
            )
        )
    got = [moved(both[k], "y", k) for k in range(1, AXIS)]
    grad_in = added(both[0], got)
    at = grad_in.shape[1] - SMALL_WIDE
    small = (small.astype(f32) + got[1][:, at:].astype(f32)) + (got[0][:, at:].astype(f32) + got[2][:, at:].astype(f32))
    flat, at, totals = small.ravel(), 0, []
    for s in smalls:
        totals.append(flat[at : at + s.size].reshape(s.shape))
        at += s.size
    wide_a = INNER + QKV
    grad_in = jnp.concatenate(
        [grad_in[:, :INNER], grad_in[:, wide_a : wide_a + CONVW + NH], grad_in[:, INNER:wide_a]], axis=1
    )
    return (
        output,
        d_tokens,
        grad_in,
        *totals[:7],
        grad_out,
        totals[7],
        ff[:, :part].T,
        ff[:, part : 2 * part].T,
        ff[:, 2 * part :],
    )


def solution(mesh):
    fine = Mesh(mesh.devices.reshape(AXIS, AXIS, AXIS, 2), ALL)
    rows = P(ALL, None)
    placed = (
        rows,
        rows,
        *((P(),) * 10),
        P("y", COL),
        P("y", COL),
        P(COL, "y"),
        rows,
    )
    return jax.shard_map(
        local,
        mesh=fine,
        in_specs=placed,
        out_specs=(
            rows,
            rows,
            rows,
            *((P(),) * 7),
            rows,
            P(),
            P("y", COL),
            P("y", COL),
            P(COL, "y"),
        ),
        check_vma=False,
    )
```

```python
import math

import jax
import jax.numpy as jnp
from jax import lax
from jax.experimental import pallas as pl
from jax.experimental.pallas import tpu as pltpu
from jax.sharding import Mesh, PartitionSpec as P

NH = 24
HEAD_SIZE = 64
NS = 128
QUERY_HEADS = 8
KEY_VALUE_HEADS = 2
INNER = NH * HEAD_SIZE
CONVW = INNER + 2 * NS
QKV = (QUERY_HEADS + 2 * KEY_VALUE_HEADS) * HEAD_SIZE

norm_eps = 1e-05
rope_base = 100000000000.0
f32 = jnp.float32
bf16 = jnp.bfloat16

ALL = ("y", "x", "z", "core")
CHIPS = ("y", "x", "z")
COL = ("x", "z", "core")
AXIS = 4


def moved(array, axis, shift):
    size = lax.axis_size(axis)
    return lax.ppermute(array, axis, [(i, (i + shift) % size) for i in range(size)])


def turned(array, axis, dim):
    twice = jnp.concatenate([array, array], axis=dim)
    return lax.dynamic_slice_in_dim(twice, lax.axis_index(axis), AXIS, axis=dim)


def added(first, others):
    total = first.astype(f32)
    for o in others:
        total = total + o.astype(f32)
    return total


def rms_norm(values, gain):
    return values * lax.rsqrt(jnp.mean(values * values, axis=-1, keepdims=True) + norm_eps) * gain


def layout(lens, token_count):
    ends = jnp.cumsum(lens)
    places = jnp.arange(token_count, dtype=jnp.int32)
    after = (places[:, None] >= ends[None, :]).astype(jnp.int32)
    segment = jnp.sum(after, axis=1)
    first = jnp.sum(after * lens[None, :], axis=1)
    return (segment, places - first)


def rotary_apply(values, cosine_table, sine_table):
    half = values.shape[-1] // 2
    front = values[..., :half]
    back = values[..., half:]
    return jnp.concatenate(
        [front * cosine_table - back * sine_table, back * cosine_table + front * sine_table],
        axis=-1,
    )


def short_conv(conv_in, conv_weight, conv_bias, segment):
    token_count, width = conv_in.shape
    taps = conv_weight.shape[0]
    summed = conv_bias + conv_weight[taps - 1] * conv_in
    for offset in range(1, taps):
        earlier = jnp.concatenate([jnp.zeros((offset, width), f32), conv_in[: token_count - offset]], axis=0)
        prior_segment = jnp.concatenate([jnp.full((offset,), -1, jnp.int32), segment[: token_count - offset]])
        keep = (prior_segment == segment).astype(f32)[:, None]
        summed = summed + conv_weight[taps - 1 - offset] * earlier * keep
    return jax.nn.silu(summed)


def state_sum(active, step_in, step_bias, decay_log, skip_gain, allowed):
    token_count = active.shape[0]
    heads_in = active[:, :INNER].reshape(token_count, NH, HEAD_SIZE)
    state_in = active[:, INNER : INNER + NS]
    state_out = active[:, INNER + NS :]
    delta = jax.nn.softplus(step_in + step_bias)
    running = jnp.cumsum(-delta * jnp.exp(decay_log), axis=0)
    spread = running.T[:, :, None] - running.T[:, None, :]
    decay = jnp.where(allowed[None], jnp.exp(jnp.where(allowed[None], spread, 0.0)), 0.0)
    intersection = jnp.dot(state_out, state_in.T)
    mixing = intersection[None] * decay * delta.T[:, None, :]
    states = jnp.einsum("hts,shp->thp", mixing, heads_in) + skip_gain[None, :, None] * heads_in
    return states.reshape(token_count, INNER)


def gated_norm(states, out_gate, ssm_gain):
    return rms_norm(states * jax.nn.silu(out_gate), ssm_gain)


def attention(attention_input, position, allowed):
    token_count = attention_input.shape[0]
    queries = QUERY_HEADS * HEAD_SIZE
    keys = queries + KEY_VALUE_HEADS * HEAD_SIZE
    query_rows = attention_input[:, :queries].reshape(token_count, QUERY_HEADS, HEAD_SIZE)
    every_key = attention_input[:, queries:keys].reshape(token_count, KEY_VALUE_HEADS, HEAD_SIZE)
    every_value = attention_input[:, keys:].reshape(token_count, KEY_VALUE_HEADS, HEAD_SIZE)
    half = HEAD_SIZE // 2
    frequency = rope_base ** (-jnp.arange(half, dtype=f32) / half)
    angles = position.astype(f32)[:, None] * frequency[None, :]
    cosine_table = jnp.cos(angles)[:, None, :]
    sine_table = jnp.sin(angles)[:, None, :]
    rotated_query = rotary_apply(query_rows, cosine_table, sine_table).reshape(
        token_count, KEY_VALUE_HEADS, QUERY_HEADS // KEY_VALUE_HEADS, HEAD_SIZE
    )
    turned_k = rotary_apply(every_key, cosine_table, sine_table)
    scores = jnp.einsum("tkgd,skd->kgts", rotated_query, turned_k) / math.sqrt(HEAD_SIZE)
    scores = jnp.where(allowed[None, None], scores, -1e30)
    attention_weights = jax.nn.softmax(scores, axis=-1)
    return jnp.einsum("kgts,skd->tkgd", attention_weights, every_value).reshape(token_count, queries)


def dot_nn(left, right):
    return lax.dot_general(left, right, (((1,), (0,)), ((), ())), preferred_element_type=f32)


def dot_nt(left, right):
    return lax.dot_general(left, right, (((1,), (1,)), ((), ())), preferred_element_type=f32)


def dot_tn(left, right):
    return lax.dot_general(left, right, (((0,), (0,)), ((), ())), preferred_element_type=f32)


FF_BLOCK = 256


def ffn_body(x_ref, x2_ref, ct_ref, ct2_ref, w_ref, out_ref, dn_ref, back_ref, dw_ref):
    @pl.when(pl.program_id(0) == 0)
    def _():
        out_ref[...] = jnp.zeros_like(out_ref)
        dn_ref[...] = jnp.zeros_like(dn_ref)
        back_ref[...] = jnp.zeros_like(back_ref)

    tokens, width = x_ref.shape
    x = jnp.concatenate([x_ref[...], x2_ref[...]], axis=0)
    ct = jnp.concatenate([ct_ref[...], ct2_ref[...]], axis=0)
    part = width // AXIS
    gate, up, d_hidden = 0.0, 0.0, 0.0
    for c in range(AXIS):
        cols = slice(c * part, (c + 1) * part)
        gate = gate + dot_nt(x[:, cols], w_ref[c, :, :part])
        up = up + dot_nt(x[:, cols], w_ref[c, :, part : 2 * part])
        d_hidden = d_hidden + dot_nt(ct[:, cols], w_ref[c, :, 2 * part :])
    sigma = jax.nn.sigmoid(gate)
    silu = gate * sigma
    hidden = (silu * up).astype(bf16)
    d_gate = (d_hidden * up * sigma * (1.0 + gate * (1.0 - sigma))).astype(bf16)
    d_up = (d_hidden * silu).astype(bf16)
    for j, (left, right) in enumerate(((d_gate, x), (d_up, x), (hidden, ct))):
        dw_ref[:, j * width : (j + 1) * width] = dot_tn(left, right).astype(bf16)
    for c in range(AXIS):
        cols = slice(c * part, (c + 1) * part)
        out = dot_nn(hidden, w_ref[c, :, 2 * part :])
        dn = dot_nn(d_gate, w_ref[c, :, :part]) + dot_nn(d_up, w_ref[c, :, part : 2 * part])
        out_ref[:, cols] += out[:tokens]
        dn_ref[:, cols] += dn[:tokens]
        back_ref[:, cols] += out[tokens:]
        back_ref[:, width + c * part : width + (c + 1) * part] += dn[tokens:]


def feed_forward(x, x2, ct, ct2, weights):
    chunks, units, wide = weights.shape
    tokens, width = x.shape
    whole = pl.BlockSpec((tokens, width), lambda i: (0, 0))
    both = pl.BlockSpec((tokens, 2 * width), lambda i: (0, 0))
    total = jax.ShapeDtypeStruct((tokens, width), f32)
    return pl.pallas_call(
        ffn_body,
        grid=(units // FF_BLOCK,),
        in_specs=[whole] * 4 + [pl.BlockSpec((chunks, FF_BLOCK, wide), lambda i: (0, i, 0))],
        out_specs=[whole, whole, both, pl.BlockSpec((FF_BLOCK, 3 * width), lambda i: (i, 0))],
        out_shape=[
            total,
            total,
            jax.ShapeDtypeStruct((tokens, 2 * width), f32),
            jax.ShapeDtypeStruct((units, 3 * width), bf16),
        ],
        compiler_params=pltpu.CompilerParams(vmem_limit_bytes=48 * 1024 * 1024),
        cost_estimate=pl.CostEstimate(
            flops=36 * tokens * width * units,
            bytes_accessed=4 * chunks * units * wide,
            transcendentals=2 * tokens * units,
        ),
        name="feed_forward",
    )(x, x2, ct, ct2, weights)


def swapped(array):
    return moved(array, "core", 1)


def sent(parts, axis):
    return [moved(parts[k], axis, k) for k in range(1, AXIS)]


def halves(array):
    blocks = array.T.reshape(AXIS, AXIS, AXIS, 2, -1, array.shape[0])
    blocks = lax.dynamic_index_in_dim(blocks, lax.axis_index("core"), 3, False)
    for dim, axis in enumerate(CHIPS):
        blocks = turned(blocks, axis, dim)
    return blocks.reshape(AXIS, -1, array.shape[0])


def fixed(small):
    return lax.optimization_barrier(small.astype(bf16))


def sum_of_small(own, got):
    a, b, c = (g.astype(f32) for g in got)
    return (own.astype(f32) + b) + (a + c)


def local(
    tokens,
    lengths,
    mixer_in,
    conv_weight,
    conv_bias,
    step_bias,
    decay_log,
    skip_gain,
    ssm_gain,
    gain_in,
    mixer_out,
    gain_mlp,
    w_gate,
    w_up,
    w_down,
    cotangent,
):
    token_count, width = tokens.shape

    own = jnp.concatenate([w_gate.T, w_up.T, w_down], axis=1)
    weights = lax.all_gather(own, CHIPS, tiled=True).reshape(AXIS, -1, own.shape[1])
    units = own.shape[0]

    segment, position = layout(lengths[0], token_count)
    first_in = tokens.astype(f32)
    normed_first, first_pull = jax.vjp(rms_norm, first_in, gain_in)
    normed_first_low = normed_first.astype(bf16)
    projected = jnp.dot(normed_first_low, mixer_in, preferred_element_type=f32)

    places = jnp.arange(token_count, dtype=jnp.int32)
    allowed = (places[:, None] >= places[None, :]) & (segment[:, None] == segment[None, :])
    active, conv_pull = jax.vjp(
        lambda v, w, b: short_conv(v, w, b, segment), projected[:, INNER : INNER + CONVW], conv_weight, conv_bias
    )
    states, state_pull = jax.vjp(
        lambda *v: state_sum(*v, allowed),
        active,
        projected[:, INNER + CONVW : INNER + CONVW + NH],
        step_bias,
        decay_log,
        skip_gain,
    )
    ssm_out, gated_pull = jax.vjp(gated_norm, states, projected[:, :INNER], ssm_gain)
    attended, attention_pull = jax.vjp(
        lambda v: attention(v, position, allowed), projected[:, INNER + CONVW + NH :]
    )
    joined_wide = jnp.concatenate([ssm_out, attended], axis=1)
    joined = joined_wide.astype(bf16)
    mixed = first_in + jnp.dot(joined, mixer_out, preferred_element_type=f32)
    normed_mlp, norm_pull = jax.vjp(rms_norm, mixed, gain_mlp)
    normed_low = normed_mlp.astype(bf16)
    ffn_out, d_normed, back, d_weights = feed_forward(
        normed_low, swapped(normed_low), cotangent, swapped(cotangent), weights
    )
    back = swapped(back)
    output = (mixed + (ffn_out + back[:, :width])).astype(bf16)
    d_normed = d_normed + back[:, width:]

    ff = lax.psum_scatter(d_weights, ("x", "z"), scatter_dimension=0, tiled=True)
    ff = turned(ff.reshape(units, 3, AXIS, -1).transpose(2, 0, 1, 3).reshape(AXIS, units, -1), "y", 0)
    ff = added(ff[0], sent(ff, "y"))
    part = ff.shape[1] // 3

    d_mixed, d_gain_mlp = norm_pull(d_normed)
    d_mixed = d_mixed + cotangent.astype(f32)
    d_term = d_mixed.astype(bf16)

    lefts = halves(jnp.concatenate([joined, swapped(joined)]))
    right = jnp.concatenate([d_term, swapped(d_term)])
    outs = [dot_nn(lefts[k], right).astype(bf16) for k in range(AXIS)]
    d_joined = dot_nt(d_term, mixer_out)
    d_joined, *outs = lax.optimization_barrier((d_joined, *outs))
    outs_got = sent(outs, "y")
    d_states, d_gate, d_ssm_gain = gated_pull(d_joined[:, :INNER])
    (d_qkv,) = attention_pull(d_joined[:, INNER:])
    d_gate, d_qkv = d_gate.astype(bf16), d_qkv.astype(bf16)
    lefts = halves(jnp.concatenate([normed_first_low, swapped(normed_first_low)]))
    right = jnp.concatenate([d_gate, d_qkv], axis=1)
    right = jnp.concatenate([right, swapped(right)])
    ins_a = [dot_nn(lefts[k], right).astype(bf16) for k in range(AXIS)]
    d_states, *ins_a = lax.optimization_barrier((d_states, *ins_a))
    got_a = sent(ins_a, "y")
    d_active, d_step, d_step_bias, d_decay_log, d_skip_gain = state_pull(d_states)
    d_conv, d_conv_weight, d_conv_bias = conv_pull(d_active)
    d_conv, d_step = d_conv.astype(bf16), d_step.astype(bf16)
    d_params = [d_conv_weight, d_conv_bias, d_step_bias, d_decay_log, d_skip_gain, d_ssm_gain]
    d_projected = jnp.concatenate([d_gate, d_conv, d_step, d_qkv], axis=1)
    d_normed_first = dot_nt(d_projected, mixer_in)
    d_first, d_gain_in = first_pull(d_normed_first)
    d_tokens = d_mixed + d_first

    spare = -(CONVW + NH) % 128
    right = jnp.concatenate([d_conv, jnp.pad(d_step, ((0, 0), (0, spare)))], axis=1)
    right, *outs_got = lax.optimization_barrier((right, *outs_got))
    grad_out = added(outs[0], outs_got).astype(bf16)
    grad_out = grad_out.reshape(AXIS**2 * 8, -1)
    right = jnp.concatenate([right, swapped(right)])
    ins_b = [dot_nn(lefts[k], right).astype(bf16) for k in range(AXIS)]
    smalls = [*d_params, d_gain_in, d_gain_mlp]
    small = jnp.concatenate([s.ravel() for s in smalls])
    small_wide = -(-small.size // 1024) * 128
    small = jnp.pad(small, (0, 8 * small_wide - small.size)).reshape(8, small_wide)
    small = fixed(small)
    small = fixed(added(small, [swapped(small)]))

    def riding(block, small):
        return jnp.concatenate([block, jnp.pad(small, ((0, 0), (0, block.shape[1] - small_wide)))])

    got_b = [moved(riding(ins_b[k], small), "y", k) for k in range(1, AXIS)]
    rows = ins_b[0].shape[0]
    small = fixed(sum_of_small(small, [g[rows:, :small_wide] for g in got_b]))
    ins = jnp.concatenate(
        [
            added(ins_a[0], got_a).astype(bf16),
            added(ins_b[0], [g[:rows] for g in got_b]).astype(bf16),
            grad_out,
        ],
        axis=1,
    )
    for axis in ("x", "z"):
        if axis == "z":
            ins, ff = lax.optimization_barrier((ins, ff))
        rows = ins.shape[0] // AXIS
        got = [moved(riding(ins[k * rows : (k + 1) * rows], small), axis, k) for k in range(1, AXIS)]
        ins = added(ins[:rows], [g[:rows] for g in got])
        small = sum_of_small(small, [g[rows:, :small_wide] for g in got])
        if axis == "x":
            ins, small = ins.astype(bf16), fixed(small)
    wide_a = INNER + QKV
    wide_b = wide_a + CONVW + NH
    grad_in = jnp.concatenate([ins[:, :INNER], ins[:, wide_a:wide_b], ins[:, INNER:wide_a]], axis=1)
    grad_out = ins[:, wide_b + spare :].reshape(-1, width)
    flat, at, totals = small.ravel(), 0, []
    for s in smalls:
        totals.append(flat[at : at + s.size].reshape(s.shape))
        at += s.size
    return (
        output,
        d_tokens,
        grad_in,
        *totals[:7],
        grad_out,
        totals[7],
        ff[:, :part].T,
        ff[:, part : 2 * part].T,
        ff[:, 2 * part :],
    )


def solution(mesh):
    fine = Mesh(mesh.devices.reshape(AXIS, AXIS, AXIS, 2), ALL)
    rows = P(ALL, None)
    placed = (
        rows,
        rows,
        *((P(),) * 10),
        P("y", COL),
        P("y", COL),
        P(COL, "y"),
        rows,
    )
    return jax.shard_map(
        local,
        mesh=fine,
        in_specs=placed,
        out_specs=(
            rows,
            rows,
            rows,
            *((P(),) * 7),
            rows,
            P(),
            P("y", COL),
            P("y", COL),
            P(COL, "y"),
        ),
        check_vma=False,
    )
```

```python
import math

import jax
import jax.numpy as jnp
from jax import lax
from jax.experimental import pallas as pl
from jax.experimental.pallas import tpu as pltpu
from jax.sharding import Mesh, PartitionSpec as P

NH = 24
HEAD_SIZE = 64
NS = 128
QUERY_HEADS = 8
KEY_VALUE_HEADS = 2
INNER = NH * HEAD_SIZE
CONVW = INNER + 2 * NS
QKV = (QUERY_HEADS + 2 * KEY_VALUE_HEADS) * HEAD_SIZE

norm_eps = 1e-05
rope_base = 100000000000.0
f32 = jnp.float32
bf16 = jnp.bfloat16

ALL = ("y", "x", "z", "core")
CHIPS = ("y", "x", "z")
COL = ("x", "z", "core")
AXIS = 4


def moved(array, axis, shift):
    size = lax.axis_size(axis)
    return lax.ppermute(array, axis, [(i, (i + shift) % size) for i in range(size)])


def turned(array, axis, dim):
    twice = jnp.concatenate([array, array], axis=dim)
    return lax.dynamic_slice_in_dim(twice, lax.axis_index(axis), AXIS, axis=dim)


def added(first, others):
    total = first.astype(f32)
    for o in others:
        total = total + o.astype(f32)
    return total


def rms_norm(values, gain):
    return values * lax.rsqrt(jnp.mean(values * values, axis=-1, keepdims=True) + norm_eps) * gain


def layout(lens, token_count):
    ends = jnp.cumsum(lens)
    places = jnp.arange(token_count, dtype=jnp.int32)
    after = (places[:, None] >= ends[None, :]).astype(jnp.int32)
    segment = jnp.sum(after, axis=1)
    first = jnp.sum(after * lens[None, :], axis=1)
    return (segment, places - first)


def rotary_apply(values, cosine_table, sine_table):
    half = values.shape[-1] // 2
    front = values[..., :half]
    back = values[..., half:]
    return jnp.concatenate(
        [front * cosine_table - back * sine_table, back * cosine_table + front * sine_table],
        axis=-1,
    )


def short_conv(conv_in, conv_weight, conv_bias, segment):
    token_count, width = conv_in.shape
    taps = conv_weight.shape[0]
    summed = conv_bias + conv_weight[taps - 1] * conv_in
    for offset in range(1, taps):
        earlier = jnp.concatenate([jnp.zeros((offset, width), f32), conv_in[: token_count - offset]], axis=0)
        prior_segment = jnp.concatenate([jnp.full((offset,), -1, jnp.int32), segment[: token_count - offset]])
        keep = (prior_segment == segment).astype(f32)[:, None]
        summed = summed + conv_weight[taps - 1 - offset] * earlier * keep
    return jax.nn.silu(summed)


def state_sum(active, step_in, step_bias, decay_log, skip_gain, allowed):
    token_count = active.shape[0]
    heads_in = active[:, :INNER].reshape(token_count, NH, HEAD_SIZE)
    state_in = active[:, INNER : INNER + NS]
    state_out = active[:, INNER + NS :]
    delta = jax.nn.softplus(step_in + step_bias)
    running = jnp.cumsum(-delta * jnp.exp(decay_log), axis=0)
    spread = running.T[:, :, None] - running.T[:, None, :]
    decay = jnp.where(allowed[None], jnp.exp(jnp.where(allowed[None], spread, 0.0)), 0.0)
    intersection = jnp.dot(state_out, state_in.T)
    mixing = intersection[None] * decay * delta.T[:, None, :]
    states = jnp.einsum("hts,shp->thp", mixing, heads_in) + skip_gain[None, :, None] * heads_in
    return states.reshape(token_count, INNER)


def gated_norm(states, out_gate, ssm_gain):
    return rms_norm(states * jax.nn.silu(out_gate), ssm_gain)


def attention(attention_input, position, allowed):
    token_count = attention_input.shape[0]
    queries = QUERY_HEADS * HEAD_SIZE
    keys = queries + KEY_VALUE_HEADS * HEAD_SIZE
    query_rows = attention_input[:, :queries].reshape(token_count, QUERY_HEADS, HEAD_SIZE)
    every_key = attention_input[:, queries:keys].reshape(token_count, KEY_VALUE_HEADS, HEAD_SIZE)
    every_value = attention_input[:, keys:].reshape(token_count, KEY_VALUE_HEADS, HEAD_SIZE)
    half = HEAD_SIZE // 2
    frequency = rope_base ** (-jnp.arange(half, dtype=f32) / half)
    angles = position.astype(f32)[:, None] * frequency[None, :]
    cosine_table = jnp.cos(angles)[:, None, :]
    sine_table = jnp.sin(angles)[:, None, :]
    rotated_query = rotary_apply(query_rows, cosine_table, sine_table).reshape(
        token_count, KEY_VALUE_HEADS, QUERY_HEADS // KEY_VALUE_HEADS, HEAD_SIZE
    )
    turned_k = rotary_apply(every_key, cosine_table, sine_table)
    scores = jnp.einsum("tkgd,skd->kgts", rotated_query, turned_k) / math.sqrt(HEAD_SIZE)
    scores = jnp.where(allowed[None, None], scores, -1e30)
    attention_weights = jax.nn.softmax(scores, axis=-1)
    return jnp.einsum("kgts,skd->tkgd", attention_weights, every_value).reshape(token_count, queries)


def dot_nn(left, right):
    return lax.dot_general(left, right, (((1,), (0,)), ((), ())), preferred_element_type=f32)


def dot_nt(left, right):
    return lax.dot_general(left, right, (((1,), (1,)), ((), ())), preferred_element_type=f32)


def dot_tn(left, right):
    return lax.dot_general(left, right, (((0,), (0,)), ((), ())), preferred_element_type=f32)


FF_BLOCK = 256


def ffn_body(x_ref, x2_ref, ct_ref, ct2_ref, w_ref, out_ref, dn_ref, back_ref, dw_ref):
    @pl.when(pl.program_id(0) == 0)
    def _():
        out_ref[...] = jnp.zeros_like(out_ref)
        dn_ref[...] = jnp.zeros_like(dn_ref)
        back_ref[...] = jnp.zeros_like(back_ref)

    tokens, width = x_ref.shape
    x = jnp.concatenate([x_ref[...], x2_ref[...]], axis=0)
    ct = jnp.concatenate([ct_ref[...], ct2_ref[...]], axis=0)
    part = width // AXIS
    gate, up, d_hidden = 0.0, 0.0, 0.0
    for c in range(AXIS):
        cols = slice(c * part, (c + 1) * part)
        gate = gate + dot_nt(x[:, cols], w_ref[c, :, :part])
        up = up + dot_nt(x[:, cols], w_ref[c, :, part : 2 * part])
        d_hidden = d_hidden + dot_nt(ct[:, cols], w_ref[c, :, 2 * part :])
    sigma = jax.nn.sigmoid(gate)
    silu = gate * sigma
    hidden = (silu * up).astype(bf16)
    d_gate = (d_hidden * up * sigma * (1.0 + gate * (1.0 - sigma))).astype(bf16)
    d_up = (d_hidden * silu).astype(bf16)
    for j, (left, right) in enumerate(((d_gate, x), (d_up, x), (hidden, ct))):
        dw_ref[:, j * width : (j + 1) * width] = dot_tn(left, right).astype(bf16)
    for c in range(AXIS):
        cols = slice(c * part, (c + 1) * part)
        out = dot_nn(hidden, w_ref[c, :, 2 * part :])
        dn = dot_nn(d_gate, w_ref[c, :, :part]) + dot_nn(d_up, w_ref[c, :, part : 2 * part])
        out_ref[:, cols] += out[:tokens]
        dn_ref[:, cols] += dn[:tokens]
        back_ref[:, cols] += out[tokens:]
        back_ref[:, width + c * part : width + (c + 1) * part] += dn[tokens:]


def feed_forward(x, x2, ct, ct2, weights):
    chunks, units, wide = weights.shape
    tokens, width = x.shape
    whole = pl.BlockSpec((tokens, width), lambda i: (0, 0))
    both = pl.BlockSpec((tokens, 2 * width), lambda i: (0, 0))
    total = jax.ShapeDtypeStruct((tokens, width), f32)
    return pl.pallas_call(
        ffn_body,
        grid=(units // FF_BLOCK,),
        in_specs=[whole] * 4 + [pl.BlockSpec((chunks, FF_BLOCK, wide), lambda i: (0, i, 0))],
        out_specs=[whole, whole, both, pl.BlockSpec((FF_BLOCK, 3 * width), lambda i: (i, 0))],
        out_shape=[
            total,
            total,
            jax.ShapeDtypeStruct((tokens, 2 * width), f32),
            jax.ShapeDtypeStruct((units, 3 * width), bf16),
        ],
        compiler_params=pltpu.CompilerParams(vmem_limit_bytes=48 * 1024 * 1024),
        cost_estimate=pl.CostEstimate(
            flops=36 * tokens * width * units,
            bytes_accessed=4 * chunks * units * wide,
            transcendentals=2 * tokens * units,
        ),
        name="feed_forward",
    )(x, x2, ct, ct2, weights)


def swapped(array):
    return moved(array, "core", 1)


def sent(parts, axis):
    return [moved(parts[k], axis, k) for k in range(1, AXIS)]


def halves(array):
    blocks = array.T.reshape(AXIS, AXIS, AXIS, 2, -1, array.shape[0])
    blocks = lax.dynamic_index_in_dim(blocks, lax.axis_index("core"), 3, False)
    for dim, axis in enumerate(CHIPS):
        blocks = turned(blocks, axis, dim)
    return blocks.reshape(AXIS, -1, array.shape[0])


def fixed(small):
    return lax.optimization_barrier(small.astype(bf16))


def sum_of_small(own, got):
    a, b, c = (g.astype(f32) for g in got)
    return (own.astype(f32) + b) + (a + c)


def local(
    tokens,
    lengths,
    mixer_in,
    conv_weight,
    conv_bias,
    step_bias,
    decay_log,
    skip_gain,
    ssm_gain,
    gain_in,
    mixer_out,
    gain_mlp,
    w_gate,
    w_up,
    w_down,
    cotangent,
):
    token_count, width = tokens.shape

    own = jnp.concatenate([w_gate.T, w_up.T, w_down], axis=1)
    weights = lax.all_gather(own, CHIPS, tiled=True).reshape(AXIS, -1, own.shape[1])
    units = own.shape[0]

    segment, position = layout(lengths[0], token_count)
    first_in = tokens.astype(f32)
    normed_first, first_pull = jax.vjp(rms_norm, first_in, gain_in)
    normed_first_low = normed_first.astype(bf16)
    projected = jnp.dot(normed_first_low, mixer_in, preferred_element_type=f32)

    places = jnp.arange(token_count, dtype=jnp.int32)
    allowed = (places[:, None] >= places[None, :]) & (segment[:, None] == segment[None, :])
    active, conv_pull = jax.vjp(
        lambda v, w, b: short_conv(v, w, b, segment), projected[:, INNER : INNER + CONVW], conv_weight, conv_bias
    )
    states, state_pull = jax.vjp(
        lambda *v: state_sum(*v, allowed),
        active,
        projected[:, INNER + CONVW : INNER + CONVW + NH],
        step_bias,
        decay_log,
        skip_gain,
    )
    ssm_out, gated_pull = jax.vjp(gated_norm, states, projected[:, :INNER], ssm_gain)
    attended, attention_pull = jax.vjp(
        lambda v: attention(v, position, allowed), projected[:, INNER + CONVW + NH :]
    )
    joined_wide = jnp.concatenate([ssm_out, attended], axis=1)
    joined = joined_wide.astype(bf16)
    mixed = first_in + jnp.dot(joined, mixer_out, preferred_element_type=f32)
    normed_mlp, norm_pull = jax.vjp(rms_norm, mixed, gain_mlp)
    normed_low = normed_mlp.astype(bf16)
    ffn_out, d_normed, back, d_weights = feed_forward(
        normed_low, swapped(normed_low), cotangent, swapped(cotangent), weights
    )
    back = swapped(back)
    output = (mixed + (ffn_out + back[:, :width])).astype(bf16)
    d_normed = d_normed + back[:, width:]

    ff = lax.psum_scatter(d_weights, ("x", "z"), scatter_dimension=0, tiled=True)
    ff = turned(ff.reshape(units, 3, AXIS, -1).transpose(2, 0, 1, 3).reshape(AXIS, units, -1), "y", 0)
    ff = added(ff[0], sent(ff, "y"))
    part = ff.shape[1] // 3

    d_mixed, d_gain_mlp = norm_pull(d_normed)
    d_mixed = d_mixed + cotangent.astype(f32)
    d_term = d_mixed.astype(bf16)

    lefts = halves(jnp.concatenate([joined, swapped(joined)]))
    right = jnp.concatenate([d_term, swapped(d_term)])
    outs = [dot_nn(lefts[k], right).astype(bf16) for k in range(AXIS)]
    d_joined = dot_nt(d_term, mixer_out)
    d_joined, *outs = lax.optimization_barrier((d_joined, *outs))
    outs_got = sent(outs, "y")
    d_states, d_gate, d_ssm_gain = gated_pull(d_joined[:, :INNER])
    (d_qkv,) = attention_pull(d_joined[:, INNER:])
    d_gate, d_qkv = d_gate.astype(bf16), d_qkv.astype(bf16)
    lefts = halves(jnp.concatenate([normed_first_low, swapped(normed_first_low)]))
    right = jnp.concatenate([d_gate, d_qkv], axis=1)
    right = jnp.concatenate([right, swapped(right)])
    ins_a = [dot_nn(lefts[k], right).astype(bf16) for k in range(AXIS)]
    d_states, *ins_a = lax.optimization_barrier((d_states, *ins_a))
    got_a = sent(ins_a, "y")
    d_active, d_step, d_step_bias, d_decay_log, d_skip_gain = state_pull(d_states)
    d_conv, d_conv_weight, d_conv_bias = conv_pull(d_active)
    d_conv, d_step = d_conv.astype(bf16), d_step.astype(bf16)
    d_params = [d_conv_weight, d_conv_bias, d_step_bias, d_decay_log, d_skip_gain, d_ssm_gain]
    d_projected = jnp.concatenate([d_gate, d_conv, d_step, d_qkv], axis=1)
    d_normed_first = dot_nt(d_projected, mixer_in)
    d_first, d_gain_in = first_pull(d_normed_first)
    d_tokens = d_mixed + d_first

    spare = -(CONVW + NH) % 128
    right = jnp.concatenate([d_conv, jnp.pad(d_step, ((0, 0), (0, spare)))], axis=1)
    right, *outs_got = lax.optimization_barrier((right, *outs_got))
    grad_out = added(outs[0], outs_got).astype(bf16)
    grad_out = grad_out.reshape(AXIS**2 * 8, -1)
    right = jnp.concatenate([right, swapped(right)])
    ins_b = [dot_nn(lefts[k], right).astype(bf16) for k in range(AXIS)]
    smalls = [*d_params, d_gain_in, d_gain_mlp]
    small = jnp.concatenate([s.ravel() for s in smalls])
    small_wide = -(-small.size // 1024) * 128
    small = jnp.pad(small, (0, 8 * small_wide - small.size)).reshape(8, small_wide)
    small = fixed(small)
    small = fixed(added(small, [swapped(small)]))

    def riding(block, small):
        return jnp.concatenate([block, jnp.pad(small, ((0, 0), (0, block.shape[1] - small_wide)))])

    got_b = [moved(riding(ins_b[k], small), "y", k) for k in range(1, AXIS)]
    rows = ins_b[0].shape[0]
    small = fixed(sum_of_small(small, [g[rows:, :small_wide] for g in got_b]))
    ins = jnp.concatenate(
        [
            added(ins_a[0], got_a).astype(bf16),
            added(ins_b[0], [g[:rows] for g in got_b]).astype(bf16),
            grad_out,
        ],
        axis=1,
    )
    for axis in ("x", "z"):
        rows = ins.shape[0] // AXIS
        parts = [riding(ins[k * rows : (k + 1) * rows], small) for k in range(AXIS)]
        if axis == "x":
            parts[3], ff = lax.optimization_barrier((parts[3], ff))
        got = sent(parts, axis)
        ins = added(ins[:rows], [g[:rows] for g in got])
        small = sum_of_small(small, [g[rows:, :small_wide] for g in got])
        if axis == "x":
            ins, small = ins.astype(bf16), fixed(small)
    wide_a = INNER + QKV
    wide_b = wide_a + CONVW + NH
    grad_in = jnp.concatenate([ins[:, :INNER], ins[:, wide_a:wide_b], ins[:, INNER:wide_a]], axis=1)
    grad_out = ins[:, wide_b + spare :].reshape(-1, width)
    flat, at, totals = small.ravel(), 0, []
    for s in smalls:
        totals.append(flat[at : at + s.size].reshape(s.shape))
        at += s.size
    return (
        output,
        d_tokens,
        grad_in,
        *totals[:7],
        grad_out,
        totals[7],
        ff[:, :part].T,
        ff[:, part : 2 * part].T,
        ff[:, 2 * part :],
    )


def solution(mesh):
    fine = Mesh(mesh.devices.reshape(AXIS, AXIS, AXIS, 2), ALL)
    rows = P(ALL, None)
    placed = (
        rows,
        rows,
        *((P(),) * 10),
        P("y", COL),
        P("y", COL),
        P(COL, "y"),
        rows,
    )
    return jax.shard_map(
        local,
        mesh=fine,
        in_specs=placed,
        out_specs=(
            rows,
            rows,
            rows,
            *((P(),) * 7),
            rows,
            P(),
            P("y", COL),
            P("y", COL),
            P(COL, "y"),
        ),
        check_vma=False,
    )
```

```python
import math

import jax
import jax.numpy as jnp
from jax import lax
from jax.experimental import pallas as pl
from jax.experimental.pallas import tpu as pltpu
from jax.sharding import Mesh, PartitionSpec as P

NH = 24
HEAD_SIZE = 64
NS = 128
QUERY_HEADS = 8
KEY_VALUE_HEADS = 2
INNER = NH * HEAD_SIZE
CONVW = INNER + 2 * NS
QKV = (QUERY_HEADS + 2 * KEY_VALUE_HEADS) * HEAD_SIZE

norm_eps = 1e-05
rope_base = 100000000000.0
f32 = jnp.float32
bf16 = jnp.bfloat16

ALL = ("y", "x", "z", "core")
CHIPS = ("y", "x", "z")
COL = ("x", "z", "core")
AXIS = 4


def moved(array, axis, shift):
    size = lax.axis_size(axis)
    return lax.ppermute(array, axis, [(i, (i + shift) % size) for i in range(size)])


def turned(array, axis, dim):
    twice = jnp.concatenate([array, array], axis=dim)
    return lax.dynamic_slice_in_dim(twice, lax.axis_index(axis), AXIS, axis=dim)


def added(first, others):
    total = first.astype(f32)
    for o in others:
        total = total + o.astype(f32)
    return total


def rms_norm(values, gain):
    return values * lax.rsqrt(jnp.mean(values * values, axis=-1, keepdims=True) + norm_eps) * gain


def layout(lens, token_count):
    ends = jnp.cumsum(lens)
    places = jnp.arange(token_count, dtype=jnp.int32)
    after = (places[:, None] >= ends[None, :]).astype(jnp.int32)
    segment = jnp.sum(after, axis=1)
    first = jnp.sum(after * lens[None, :], axis=1)
    return (segment, places - first)


def rotary_apply(values, cosine_table, sine_table):
    half = values.shape[-1] // 2
    front = values[..., :half]
    back = values[..., half:]
    return jnp.concatenate(
        [front * cosine_table - back * sine_table, back * cosine_table + front * sine_table],
        axis=-1,
    )


def short_conv(conv_in, conv_weight, conv_bias, segment):
    token_count, width = conv_in.shape
    taps = conv_weight.shape[0]
    summed = conv_bias + conv_weight[taps - 1] * conv_in
    for offset in range(1, taps):
        earlier = jnp.concatenate([jnp.zeros((offset, width), f32), conv_in[: token_count - offset]], axis=0)
        prior_segment = jnp.concatenate([jnp.full((offset,), -1, jnp.int32), segment[: token_count - offset]])
        keep = (prior_segment == segment).astype(f32)[:, None]
        summed = summed + conv_weight[taps - 1 - offset] * earlier * keep
    return jax.nn.silu(summed)


def state_sum(active, step_in, step_bias, decay_log, skip_gain, allowed):
    token_count = active.shape[0]
    heads_in = active[:, :INNER].reshape(token_count, NH, HEAD_SIZE)
    state_in = active[:, INNER : INNER + NS]
    state_out = active[:, INNER + NS :]
    delta = jax.nn.softplus(step_in + step_bias)
    running = jnp.cumsum(-delta * jnp.exp(decay_log), axis=0)
    spread = running.T[:, :, None] - running.T[:, None, :]
    decay = jnp.where(allowed[None], jnp.exp(jnp.where(allowed[None], spread, 0.0)), 0.0)
    intersection = jnp.dot(state_out, state_in.T)
    mixing = intersection[None] * decay * delta.T[:, None, :]
    states = jnp.einsum("hts,shp->thp", mixing, heads_in) + skip_gain[None, :, None] * heads_in
    return states.reshape(token_count, INNER)


def gated_norm(states, out_gate, ssm_gain):
    return rms_norm(states * jax.nn.silu(out_gate), ssm_gain)


def attention(attention_input, position, allowed):
    token_count = attention_input.shape[0]
    queries = QUERY_HEADS * HEAD_SIZE
    keys = queries + KEY_VALUE_HEADS * HEAD_SIZE
    query_rows = attention_input[:, :queries].reshape(token_count, QUERY_HEADS, HEAD_SIZE)
    every_key = attention_input[:, queries:keys].reshape(token_count, KEY_VALUE_HEADS, HEAD_SIZE)
    every_value = attention_input[:, keys:].reshape(token_count, KEY_VALUE_HEADS, HEAD_SIZE)
    half = HEAD_SIZE // 2
    frequency = rope_base ** (-jnp.arange(half, dtype=f32) / half)
    angles = position.astype(f32)[:, None] * frequency[None, :]
    cosine_table = jnp.cos(angles)[:, None, :]
    sine_table = jnp.sin(angles)[:, None, :]
    rotated_query = rotary_apply(query_rows, cosine_table, sine_table).reshape(
        token_count, KEY_VALUE_HEADS, QUERY_HEADS // KEY_VALUE_HEADS, HEAD_SIZE
    )
    turned_k = rotary_apply(every_key, cosine_table, sine_table)
    scores = jnp.einsum("tkgd,skd->kgts", rotated_query, turned_k) / math.sqrt(HEAD_SIZE)
    scores = jnp.where(allowed[None, None], scores, -1e30)
    attention_weights = jax.nn.softmax(scores, axis=-1)
    return jnp.einsum("kgts,skd->tkgd", attention_weights, every_value).reshape(token_count, queries)


def dot_nn(left, right):
    return lax.dot_general(left, right, (((1,), (0,)), ((), ())), preferred_element_type=f32)


def dot_nt(left, right):
    return lax.dot_general(left, right, (((1,), (1,)), ((), ())), preferred_element_type=f32)


def dot_tn(left, right):
    return lax.dot_general(left, right, (((0,), (0,)), ((), ())), preferred_element_type=f32)


FF_BLOCK = 256


def ffn_body(x_ref, x2_ref, ct_ref, ct2_ref, w_ref, out_ref, dn_ref, back_ref, dw_ref):
    @pl.when(pl.program_id(0) == 0)
    def _():
        out_ref[...] = jnp.zeros_like(out_ref)
        dn_ref[...] = jnp.zeros_like(dn_ref)
        back_ref[...] = jnp.zeros_like(back_ref)

    tokens, width = x_ref.shape
    x = jnp.concatenate([x_ref[...], x2_ref[...]], axis=0)
    ct = jnp.concatenate([ct_ref[...], ct2_ref[...]], axis=0)
    part = width // AXIS
    gate, up, d_hidden = 0.0, 0.0, 0.0
    for c in range(AXIS):
        cols = slice(c * part, (c + 1) * part)
        gate = gate + dot_nt(x[:, cols], w_ref[c, :, :part])
        up = up + dot_nt(x[:, cols], w_ref[c, :, part : 2 * part])
        d_hidden = d_hidden + dot_nt(ct[:, cols], w_ref[c, :, 2 * part :])
    sigma = jax.nn.sigmoid(gate)
    silu = gate * sigma
    hidden = (silu * up).astype(bf16)
    d_gate = (d_hidden * up * sigma * (1.0 + gate * (1.0 - sigma))).astype(bf16)
    d_up = (d_hidden * silu).astype(bf16)
    for j, (left, right) in enumerate(((d_gate, x), (d_up, x), (hidden, ct))):
        dw_ref[:, j * width : (j + 1) * width] = dot_tn(left, right).astype(bf16)
    for c in range(AXIS):
        cols = slice(c * part, (c + 1) * part)
        out = dot_nn(hidden, w_ref[c, :, 2 * part :])
        dn = dot_nn(d_gate, w_ref[c, :, :part]) + dot_nn(d_up, w_ref[c, :, part : 2 * part])
        out_ref[:, cols] += out[:tokens]
        dn_ref[:, cols] += dn[:tokens]
        back_ref[:, cols] += out[tokens:]
        back_ref[:, width + c * part : width + (c + 1) * part] += dn[tokens:]


def feed_forward(x, x2, ct, ct2, weights):
    chunks, units, wide = weights.shape
    tokens, width = x.shape
    whole = pl.BlockSpec((tokens, width), lambda i: (0, 0))
    both = pl.BlockSpec((tokens, 2 * width), lambda i: (0, 0))
    total = jax.ShapeDtypeStruct((tokens, width), f32)
    return pl.pallas_call(
        ffn_body,
        grid=(units // FF_BLOCK,),
        in_specs=[whole] * 4 + [pl.BlockSpec((chunks, FF_BLOCK, wide), lambda i: (0, i, 0))],
        out_specs=[whole, whole, both, pl.BlockSpec((FF_BLOCK, 3 * width), lambda i: (i, 0))],
        out_shape=[
            total,
            total,
            jax.ShapeDtypeStruct((tokens, 2 * width), f32),
            jax.ShapeDtypeStruct((units, 3 * width), bf16),
        ],
        compiler_params=pltpu.CompilerParams(vmem_limit_bytes=48 * 1024 * 1024),
        cost_estimate=pl.CostEstimate(
            flops=36 * tokens * width * units,
            bytes_accessed=4 * chunks * units * wide,
            transcendentals=2 * tokens * units,
        ),
        name="feed_forward",
    )(x, x2, ct, ct2, weights)


def swapped(array):
    return moved(array, "core", 1)


def sent(parts, axis):
    return [moved(parts[k], axis, k) for k in range(1, AXIS)]


def halves(array):
    blocks = array.T.reshape(AXIS, AXIS, AXIS, 2, -1, array.shape[0])
    blocks = lax.dynamic_index_in_dim(blocks, lax.axis_index("core"), 3, False)
    for dim, axis in enumerate(CHIPS):
        blocks = turned(blocks, axis, dim)
    return blocks.reshape(AXIS, -1, array.shape[0])


def fixed(small):
    return lax.optimization_barrier(small.astype(bf16))


def sum_of_small(own, got):
    a, b, c = (g.astype(f32) for g in got)
    return (own.astype(f32) + b) + (a + c)


def local(
    tokens,
    lengths,
    mixer_in,
    conv_weight,
    conv_bias,
    step_bias,
    decay_log,
    skip_gain,
    ssm_gain,
    gain_in,
    mixer_out,
    gain_mlp,
    w_gate,
    w_up,
    w_down,
    cotangent,
):
    token_count, width = tokens.shape

    own = jnp.concatenate([w_gate.T, w_up.T, w_down], axis=1)
    weights = lax.all_gather(own, CHIPS, tiled=True).reshape(AXIS, -1, own.shape[1])
    units = own.shape[0]

    segment, position = layout(lengths[0], token_count)
    first_in = tokens.astype(f32)
    normed_first, first_pull = jax.vjp(rms_norm, first_in, gain_in)
    normed_first_low = normed_first.astype(bf16)
    projected = jnp.dot(normed_first_low, mixer_in, preferred_element_type=f32)

    places = jnp.arange(token_count, dtype=jnp.int32)
    allowed = (places[:, None] >= places[None, :]) & (segment[:, None] == segment[None, :])
    active, conv_pull = jax.vjp(
        lambda v, w, b: short_conv(v, w, b, segment), projected[:, INNER : INNER + CONVW], conv_weight, conv_bias
    )
    states, state_pull = jax.vjp(
        lambda *v: state_sum(*v, allowed),
        active,
        projected[:, INNER + CONVW : INNER + CONVW + NH],
        step_bias,
        decay_log,
        skip_gain,
    )
    ssm_out, gated_pull = jax.vjp(gated_norm, states, projected[:, :INNER], ssm_gain)
    attended, attention_pull = jax.vjp(
        lambda v: attention(v, position, allowed), projected[:, INNER + CONVW + NH :]
    )
    joined_wide = jnp.concatenate([ssm_out, attended], axis=1)
    joined = joined_wide.astype(bf16)
    mixed = first_in + jnp.dot(joined, mixer_out, preferred_element_type=f32)
    normed_mlp, norm_pull = jax.vjp(rms_norm, mixed, gain_mlp)
    normed_low = normed_mlp.astype(bf16)
    ffn_out, d_normed, back, d_weights = feed_forward(
        normed_low, swapped(normed_low), cotangent, swapped(cotangent), weights
    )
    back = swapped(back)
    output = (mixed + (ffn_out + back[:, :width])).astype(bf16)
    d_normed = d_normed + back[:, width:]

    ff = lax.psum_scatter(d_weights, ("x", "z"), scatter_dimension=0, tiled=True)
    ff = turned(ff.reshape(units, 3, AXIS, -1).transpose(2, 0, 1, 3).reshape(AXIS, units, -1), "y", 0)
    ff = added(ff[0], sent(ff, "y"))
    part = ff.shape[1] // 3

    d_mixed, d_gain_mlp = norm_pull(d_normed)
    d_mixed = d_mixed + cotangent.astype(f32)
    d_term = d_mixed.astype(bf16)

    lefts = halves(jnp.concatenate([joined, swapped(joined)]))
    right = jnp.concatenate([d_term, swapped(d_term)])
    outs = [dot_nn(lefts[k], right).astype(bf16) for k in range(AXIS)]
    d_joined = dot_nt(d_term, mixer_out)
    d_joined, *outs = lax.optimization_barrier((d_joined, *outs))
    outs_got = sent(outs, "y")
    d_states, d_gate, d_ssm_gain = gated_pull(d_joined[:, :INNER])
    (d_qkv,) = attention_pull(d_joined[:, INNER:])
    d_gate, d_qkv = d_gate.astype(bf16), d_qkv.astype(bf16)
    lefts = halves(jnp.concatenate([normed_first_low, swapped(normed_first_low)]))
    right = jnp.concatenate([d_gate, d_qkv], axis=1)
    right = jnp.concatenate([right, swapped(right)])
    ins_a = [dot_nn(lefts[k], right).astype(bf16) for k in range(AXIS)]
    d_states, *ins_a = lax.optimization_barrier((d_states, *ins_a))
    got_a = sent(ins_a, "y")
    d_active, d_step, d_step_bias, d_decay_log, d_skip_gain = state_pull(d_states)
    d_conv, d_conv_weight, d_conv_bias = conv_pull(d_active)
    d_conv, d_step = d_conv.astype(bf16), d_step.astype(bf16)
    d_params = [d_conv_weight, d_conv_bias, d_step_bias, d_decay_log, d_skip_gain, d_ssm_gain]
    d_projected = jnp.concatenate([d_gate, d_conv, d_step, d_qkv], axis=1)
    d_normed_first = dot_nt(d_projected, mixer_in)
    d_first, d_gain_in = first_pull(d_normed_first)
    d_tokens = d_mixed + d_first

    spare = -(CONVW + NH) % 128
    right = jnp.concatenate([d_conv, jnp.pad(d_step, ((0, 0), (0, spare)))], axis=1)
    right, *outs_got = lax.optimization_barrier((right, *outs_got))
    grad_out = added(outs[0], outs_got).astype(bf16)
    grad_out = grad_out.reshape(AXIS**2 * 8, -1)
    right = jnp.concatenate([right, swapped(right)])
    ins_b = [dot_nn(lefts[k], right).astype(bf16) for k in range(AXIS)]
    smalls = [*d_params, d_gain_in, d_gain_mlp]
    small = jnp.concatenate([s.ravel() for s in smalls])
    small_wide = -(-small.size // 1024) * 128
    small = jnp.pad(small, (0, 8 * small_wide - small.size)).reshape(8, small_wide)
    small = fixed(small)
    small = fixed(added(small, [swapped(small)]))

    def riding(block, small):
        return jnp.concatenate([block, jnp.pad(small, ((0, 0), (0, block.shape[1] - small_wide)))])

    got_b = [moved(riding(ins_b[k], small), "y", k) for k in range(1, AXIS)]
    rows = ins_b[0].shape[0]
    small = fixed(sum_of_small(small, [g[rows:, :small_wide] for g in got_b]))
    ins = jnp.concatenate(
        [
            added(ins_a[0], got_a).astype(bf16),
            added(ins_b[0], [g[:rows] for g in got_b]).astype(bf16),
            grad_out,
        ],
        axis=1,
    )
    ins, ff = lax.optimization_barrier((ins, ff))
    for axis in ("x", "z"):
        rows = ins.shape[0] // AXIS
        got = [moved(riding(ins[k * rows : (k + 1) * rows], small), axis, k) for k in range(1, AXIS)]
        ins = added(ins[:rows], [g[:rows] for g in got])
        small = sum_of_small(small, [g[rows:, :small_wide] for g in got])
        if axis == "x":
            ins, small = ins.astype(bf16), fixed(small)
    wide_a = INNER + QKV
    wide_b = wide_a + CONVW + NH
    grad_in = jnp.concatenate([ins[:, :INNER], ins[:, wide_a:wide_b], ins[:, INNER:wide_a]], axis=1)
    grad_out = ins[:, wide_b + spare :].reshape(-1, width)
    flat, at, totals = small.ravel(), 0, []
    for s in smalls:
        totals.append(flat[at : at + s.size].reshape(s.shape))
        at += s.size
    return (
        output,
        d_tokens,
        grad_in,
        *totals[:7],
        grad_out,
        totals[7],
        ff[:, :part].T,
        ff[:, part : 2 * part].T,
        ff[:, 2 * part :],
    )


def solution(mesh):
    fine = Mesh(mesh.devices.reshape(AXIS, AXIS, AXIS, 2), ALL)
    rows = P(ALL, None)
    placed = (
        rows,
        rows,
        *((P(),) * 10),
        P("y", COL),
        P("y", COL),
        P(COL, "y"),
        rows,
    )
    return jax.shard_map(
        local,
        mesh=fine,
        in_specs=placed,
        out_specs=(
            rows,
            rows,
            rows,
            *((P(),) * 7),
            rows,
            P(),
            P("y", COL),
            P("y", COL),
            P(COL, "y"),
        ),
        check_vma=False,
    )
```
